256 devices in a mesh: dp: 4 (over y), ctx: 16 (over z, core), tp: 4 (over x).
Axes of the slice: x: 4, y: 4, z: 8, core: 2. Of those that a mesh axis runs over, the one named last changes fastest.
Arguments:
- tokens: bfloat16 [32768, 4096], P(('dp', 'ctx')), may hold values from -250 to 250
- lengths: int32 [4, 8], P('dp'), may hold values from 1 to 4096, 8192 in all within a row
- w_query: bfloat16 [4096, 2048], P(('dp', 'ctx'), 'tp'), may hold values from -0.234375 to 0.234375
- w_key: bfloat16 [4096, 512], P(('dp', 'ctx'), 'tp'), may hold values from -0.234375 to 0.234375
- value_weight: bfloat16 [4096, 512], P(('dp', 'ctx'), 'tp'), may hold values from -0.09375 to 0.09375
- w_out: bfloat16 [2048, 4096], P(None, 'tp'), may hold values from -0.125 to 0.125
Outputs:
- attended: bfloat16 [32768, 4096], P(('dp', 'ctx'), 'tp')
The draws below stay inside these ranges and needn't reach their ends.
Inputs may be any that keep to these rules, and one draw needn't show every extreme that they name: `lengths`: row b gives the 8 documents packed in order into packed row b; they sum to 8192, and in every row the longest is half of 8192.
All inputs are finite; a program needn't handle non-finite values.
Results may differ from the reference program's by a relative error of at most 0.014.
The reference program's roundings to bfloat16 on the way count: a program that leaves them out, or rounds other values in their place, can miss the bound.
Values may be sent and summed in bfloat16 or wider, within the bound.
No kernel may reach another device: no remote copies, remote signals or barrier semaphores. Data moves between devices by JAX's collectives and lax.ppermute only.
A program may use at most 64 MiB of HBM per device.

```python
import math
import jax
import jax.numpy as jnp
import numpy as np
from jax import lax

MODEL_WIDTH = 4096
HEAD_SIZE = 128
QUERY_HEADS = 16
KEY_VALUE_HEADS = 4
DOCS = 8
PACKED_LENGTH = 8192
TOKENS = 32768
N_DP = 4


def draw_tokens(key, part):
    key = jax.random.fold_in(key, 11)
    base_key, row_key, col_key = jax.random.split(key, 3)
    row_scale = jnp.exp(jax.random.uniform(row_key, (TOKENS, 1), minval=0.0, maxval=math.log(10.0)))
    col_scale = jnp.exp(jax.random.uniform(col_key, (1, MODEL_WIDTH), minval=math.log(0.5), maxval=math.log(2.0)))
    col_scale = col_scale * jnp.exp(math.log(3.0) * jnp.arange(MODEL_WIDTH, dtype=jnp.float32)[None, :] / MODEL_WIDTH)
    value_matrix = jax.random.truncated_normal(base_key, -4.0, 4.0, (TOKENS, MODEL_WIDTH)) * row_scale * col_scale
    return value_matrix.astype(jnp.bfloat16)


def draw_w_query(key, part):
    key = jax.random.fold_in(key, 23)
    value_matrix = jax.random.truncated_normal(key, -4.0, 4.0, (MODEL_WIDTH, QUERY_HEADS * HEAD_SIZE)) * 2.2 / math.sqrt(MODEL_WIDTH)
    return value_matrix.astype(jnp.bfloat16)


def draw_w_key(key, part):
    key = jax.random.fold_in(key, 29)
    value_matrix = jax.random.truncated_normal(key, -4.0, 4.0, (MODEL_WIDTH, KEY_VALUE_HEADS * HEAD_SIZE)) * 2.2 / math.sqrt(MODEL_WIDTH)
    return value_matrix.astype(jnp.bfloat16)


def level_of(stream_key, shape, shards, smallest, top_value):
    level, own = 1.0, jax.random.fold_in(stream_key, 6)
    for axis_at, parts in shards:
        heights = jnp.exp(jax.random.uniform(jax.random.fold_in(own, axis_at), (parts,), jnp.float32, smallest / len(shards), top_value / len(shards)))
        level = level * jnp.repeat(heights, shape[axis_at] // parts).reshape([-1 if axis == axis_at else 1 for axis in range(len(shape))])
    return level


def profile(number_of, total, bound, skew):
    portions = [(1 << 20) // math.isqrt(standing ** skew) + 1 for standing in range(2, number_of + 1)]
    rest, given = total - bound - (number_of - 1), [1] * (number_of - 1)
    while rest > 0:
        candidates = [i for i in range(number_of - 1) if given[i] < bound]
        whole, remaining = sum([portions[i] for i in candidates]), rest
        for i in candidates:
            addition = min(bound - given[i], max(1, remaining * portions[i] // whole), rest)
            given[i] = given[i] + addition
            rest = rest - addition
    return np.array([bound] + given)


def uneven_parts(key, count, total, reach, lean):
    if count == 2:
        one = jax.random.randint(key, (), max(1, total - reach), min(reach, total - 1) + 1)
        return jnp.stack([one, total - one])
    sizes = jnp.asarray(profile(count, total, reach, lean), jnp.int32)
    pairs = (count - 1) // 2
    donor, sink = sizes[1:1 + 2 * pairs:2], sizes[2:2 + 2 * pairs:2]
    room = jnp.minimum(donor - 1, reach - sink)
    shifted = jax.random.randint(jax.random.fold_in(key, 1), (pairs,), 0, 1 << 20) % (room + 1)
    sizes = sizes.at[1:1 + 2 * pairs:2].set(donor - shifted).at[2:2 + 2 * pairs:2].set(sink + shifted)
    return sizes[jax.random.permutation(jax.random.fold_in(key, 2), count)]


def noise(stream_key, extent, deviation, reach, pieces=(), held_as=jnp.bfloat16):
    values = deviation * jax.random.normal(stream_key, extent, jnp.float32)
    if pieces:
        values = values * level_of(stream_key, extent, pieces, -0.22, 0.18)
    return jnp.clip(values, -reach, reach).astype(held_as)


def setup_inputs(seed: int = 0) -> dict:
    splits = jax.random.split(jax.random.key(seed), 7)
    return {
        "tokens": draw_tokens(jax.random.fold_in(splits[6], 71), 0),
        "lengths": jax.vmap(lambda own: uneven_parts(own, DOCS, PACKED_LENGTH, PACKED_LENGTH // 2, 2))(jax.random.split(splits[1], N_DP)).reshape((N_DP, DOCS)).astype(jnp.int32),
        "w_query": draw_w_query(jax.random.fold_in(splits[6], 71), 0),
        "w_key": draw_w_key(jax.random.fold_in(splits[6], 71), 0),
        "value_weight": noise(splits[4], (MODEL_WIDTH, KEY_VALUE_HEADS * HEAD_SIZE), MODEL_WIDTH ** -0.5, 0.09375, ((0, 64), (1, 4))),
        "w_out": noise(splits[5], (QUERY_HEADS * HEAD_SIZE, MODEL_WIDTH), (QUERY_HEADS * HEAD_SIZE) ** -0.5, 0.125, ((1, 4),)),
    }


EPSILON = 1e-05
MASKED_SCORE = -1e+30

def attend_row(query_matrix, projected_keys, projected_values, doc_lengths):
    queries_per_group = QUERY_HEADS // KEY_VALUE_HEADS
    score_scale = HEAD_SIZE ** (-0.5)
    doc_ends = jnp.cumsum(doc_lengths).astype(jnp.int32)
    positions = jnp.arange(PACKED_LENGTH, dtype=jnp.int32)
    doc_starts = lax.optimization_barrier(jnp.sum(jnp.where(doc_ends[None, :] <= positions[:, None], doc_lengths[None, :], 0), axis=1)).astype(jnp.int32)
    rows_per_block = min(PACKED_LENGTH, 256)
    block_list = PACKED_LENGTH // rows_per_block
    blocked_queries = query_matrix.reshape(block_list, rows_per_block, KEY_VALUE_HEADS, queries_per_group, HEAD_SIZE)
    expanded_keys = projected_keys.reshape(PACKED_LENGTH, KEY_VALUE_HEADS, HEAD_SIZE).astype(jnp.float32)
    expanded_values = projected_values.reshape(PACKED_LENGTH, KEY_VALUE_HEADS, HEAD_SIZE).astype(jnp.float32)

    def attend_block(inputs):
        query_block, query_pos, query_start = inputs
        scores = jnp.einsum('qhgd,khd->hgqk', query_block.astype(jnp.float32), expanded_keys, precision=lax.Precision.HIGHEST) * score_scale
        allowed = (positions[None, :] <= query_pos[:, None]) & (positions[None, :] >= query_start[:, None])
        scores = jnp.where(allowed, scores, MASKED_SCORE)
        row_max = lax.optimization_barrier(jnp.max(scores, axis=-1, keepdims=True))
        weights = jnp.where(allowed, jnp.exp(scores - row_max), 0.0)
        row_sum = lax.optimization_barrier(jnp.sum(weights, axis=-1))
        rounded = lax.optimization_barrier(weights.astype(jnp.bfloat16))
        blended = jnp.einsum('hgqk,khd->qhgd', rounded.astype(jnp.float32), expanded_values, precision=lax.Precision.HIGHEST)
        blended = blended / jnp.transpose(row_sum, (2, 0, 1))[..., None]
        return blended.astype(jnp.bfloat16)
    outputs = lax.map(attend_block, (blocked_queries, positions.reshape(block_list, rows_per_block), doc_starts.reshape(block_list, rows_per_block)))
    return outputs.reshape(PACKED_LENGTH, QUERY_HEADS * HEAD_SIZE)

def reference(tokens, lengths, w_query, w_key, value_weight, w_out):
    widened = tokens.astype(jnp.float32)
    normed = (widened * lax.rsqrt(lax.optimization_barrier(jnp.mean(widened * widened, axis=1, keepdims=True)) + EPSILON)).astype(jnp.bfloat16)
    query_matrix = jnp.dot(normed, w_query, preferred_element_type=jnp.float32).astype(jnp.bfloat16)
    projected_keys = jnp.dot(normed, w_key, preferred_element_type=jnp.float32).astype(jnp.bfloat16)
    projected_values = jnp.dot(normed, value_weight, preferred_element_type=jnp.float32).astype(jnp.bfloat16)

    def single_row(inputs):
        return attend_row(inputs[0], inputs[1], inputs[2], inputs[3])
    head_result = lax.map(single_row, (query_matrix.reshape(N_DP, PACKED_LENGTH, QUERY_HEADS * HEAD_SIZE), projected_keys.reshape(N_DP, PACKED_LENGTH, KEY_VALUE_HEADS * HEAD_SIZE), projected_values.reshape(N_DP, PACKED_LENGTH, KEY_VALUE_HEADS * HEAD_SIZE), lengths))
    head_result = head_result.reshape(TOKENS, QUERY_HEADS * HEAD_SIZE)
    return jnp.dot(head_result, w_out, preferred_element_type=jnp.float32).astype(jnp.bfloat16)
```

```python
import functools

import jax
import jax.numpy as jnp
from jax import lax
from jax.experimental import pallas as pl
from jax.experimental.pallas import tpu as pltpu
from jax.sharding import PartitionSpec as P

HEAD = 128
GROUP = 4
EPSILON = 1e-05
MASKED = -1e30
LOG2E = 1.4426950408889634
NZ = 8
NY = 4
NX = 4
BACK = 4
ROWS = 512
CHIP = 2 * ROWS
TQ = 256
TK = 512


def z_shift(x, step, wrap=True):
    pairs = []
    for z in range(NZ):
        to = z + step
        if wrap:
            to %= NZ
        if 0 <= to < NZ:
            pairs += [(2 * z, 2 * to), (2 * z + 1, 2 * to + 1)]
    return lax.ppermute(x, "ctx", pairs)


def swap(x):
    return lax.ppermute(x, "ctx", [(c, c ^ 1) for c in range(2 * NZ)])


def shift(x, axis, step, n):
    return lax.ppermute(x, axis, [(i, (i + step) % n) for i in range(n)])


def z_gather(piece):
    half = piece.shape[0] // 2
    f1, b1 = z_shift(piece, 1), z_shift(piece, -1)
    f2, b2 = z_shift(f1, 1), z_shift(b1, -1)
    f3, b3 = z_shift(f2, 1), z_shift(b2, -1)
    f4, b4 = z_shift(f3[:half], 1), z_shift(b3[half:], -1)
    return jnp.concatenate([piece, b1, b2, b3, f4, b4, f3, f2, f1], axis=0)


def ring4(chunk, axis):
    half = chunk.shape[0] // 2
    f1, b1 = shift(chunk, axis, 1, 4), shift(chunk, axis, -1, 4)
    f2, b2 = shift(f1[:half], axis, 1, 4), shift(b1[half:], axis, -1, 4)
    return chunk, b1, f2, b2, f1


def norm_kernel(where_ref, x_ref, o_ref):
    x = x_ref[...].astype(jnp.float32)
    scale = lax.rsqrt(jnp.mean(x * x, axis=1, keepdims=True) + EPSILON)
    y, z = where_ref[0], where_ref[1]
    for dy in range(NY):
        for dz in range(NZ):
            source = lax.rem(y + dy, NY) * NZ + lax.rem(z + dz, NZ)
            cols = pl.ds(pl.multiple_of(source * 128, 128), 128)
            out = dy * NZ + dz
            o_ref[:, out * 128:(out + 1) * 128] = (
                x_ref[:, cols].astype(jnp.float32) * scale
            ).astype(jnp.bfloat16)


def norm(tokens, where):
    rows, width = tokens.shape
    tile = 64
    return pl.pallas_call(
        norm_kernel,
        out_shape=jax.ShapeDtypeStruct((rows, width), jnp.bfloat16),
        grid=(rows // tile,),
        in_specs=[
            pl.BlockSpec(memory_space=pltpu.SMEM),
            pl.BlockSpec((tile, width), lambda i: (i, 0)),
        ],
        out_specs=pl.BlockSpec((tile, width), lambda i: (i, 0)),
        compiler_params=pltpu.CompilerParams(vmem_limit_bytes=16 << 20),
        name="norm",
    )(where, tokens)


def attend_kernel(where_ref, lengths_ref, q_ref, *refs):
    pieces, (o_ref, k_win, v_win, m_ref, l_ref, acc_ref, start_ref, sems) = refs[:20], refs[20:]
    core, z = where_ref[2], where_ref[1]
    copies = []
    for dz in range(BACK + 1):
        for which in range(2):
            side = core if which == 0 else 1 - core
            row = pl.multiple_of((BACK - dz) * CHIP + side * ROWS, ROWS)
            for kv, win in enumerate((k_win, v_win)):
                copies.append(
                    pltpu.make_async_copy(
                        pieces[dz * 4 + which * 2 + kv],
                        win.at[pl.ds(row, ROWS), :],
                        sems.at[dz * 4 + which * 2 + kv],
                    )
                )
    for copy in copies:
        copy.start()
    for copy in copies:
        copy.wait()
    base = (z - BACK) * CHIP
    factor = HEAD ** (-0.5) * LOG2E

    def start_of(pos):
        start, end = jnp.zeros_like(pos), jnp.int32(0)
        for d in range(8):
            end = end + lengths_ref[0, d]
            start = jnp.where(end <= pos, end, start)
        return start

    def scalar_start(pos):
        start, end = jnp.int32(0), jnp.int32(0)
        for d in range(8):
            end = end + lengths_ref[0, d]
            start = jnp.where(end <= pos, end, start)
        return start

    for t in range(ROWS // TQ):
        first = BACK * CHIP + core * ROWS + t * TQ
        pos = first + lax.broadcasted_iota(jnp.int32, (TQ, HEAD), 0)
        start_ref[...] = start_of(pos + base) - base
        lo = scalar_start(first + base) - base
        hi = scalar_start(first + TQ - 1 + base) - base
        m_ref[...] = jnp.full_like(m_ref, MASKED)
        l_ref[...] = jnp.zeros_like(l_ref)
        acc_ref[...] = jnp.zeros_like(acc_ref)

        def step(j, masked):
            rows = pl.ds(pl.multiple_of(j * TK, TK), TK)
            k, v = k_win[rows, :], v_win[rows, :]
            if masked:
                key = j * TK + lax.broadcasted_iota(jnp.int32, (TQ, TK), 1)
                query = first + lax.broadcasted_iota(jnp.int32, (TQ, TK), 0)
                allowed = (key <= query) & (key >= start_ref[:, :1])
            for h in range(GROUP):
                q = q_ref[t * TQ:(t + 1) * TQ, h * HEAD:(h + 1) * HEAD]
                s = lax.dot_general(q, k, (((1,), (1,)), ((), ())), preferred_element_type=jnp.float32)
                if masked:
                    s = jnp.where(allowed, s, MASKED)
                old = m_ref[h]
                new = jnp.maximum(old, jnp.max(s, axis=1, keepdims=True))
                m_ref[h] = new
                p = jnp.exp2((s - new[:, :1]) * factor)
                alpha = jnp.exp2((old - new) * factor)
                part = p[:, :HEAD]
                for i in range(1, TK // HEAD):
                    part = part + p[:, i * HEAD:(i + 1) * HEAD]
                l_ref[h] = l_ref[h] * alpha + part
                acc_ref[h] = acc_ref[h] * alpha + jnp.dot(
                    p.astype(jnp.bfloat16), v, preferred_element_type=jnp.float32
                )

        diagonal = first // TK
        stop = (first + TQ - 1) // TK + 1

        def body(j, carry):
            needs = (j >= diagonal) | (j * TK < hi)

            @pl.when(needs)
            def _():
                step(j, True)

            @pl.when(jnp.logical_not(needs))
            def _():
                step(j, False)

            return carry

        lax.fori_loop(lo // TK, stop, body, 0)
        for h in range(GROUP):
            total = jnp.sum(l_ref[h], axis=1, keepdims=True)
            o_ref[t * TQ:(t + 1) * TQ, h * HEAD:(h + 1) * HEAD] = (acc_ref[h] / total).astype(jnp.bfloat16)


def attend(where, lengths, queries, pieces):
    window = (BACK + 1) * CHIP
    return pl.pallas_call(
        attend_kernel,
        out_shape=jax.ShapeDtypeStruct(queries.shape, jnp.bfloat16),
        in_specs=[
            pl.BlockSpec(memory_space=pltpu.SMEM),
            pl.BlockSpec(memory_space=pltpu.SMEM),
            pl.BlockSpec(memory_space=pltpu.VMEM),
        ] + [pl.BlockSpec(memory_space=pl.ANY)] * len(pieces),
        out_specs=pl.BlockSpec(memory_space=pltpu.VMEM),
        scratch_shapes=[
            pltpu.VMEM((window, HEAD), jnp.bfloat16),
            pltpu.VMEM((window, HEAD), jnp.bfloat16),
            pltpu.VMEM((GROUP, TQ, HEAD), jnp.float32),
            pltpu.VMEM((GROUP, TQ, HEAD), jnp.float32),
            pltpu.VMEM((GROUP, TQ, HEAD), jnp.float32),
            pltpu.VMEM((TQ, HEAD), jnp.int32),
            pltpu.SemaphoreType.DMA((len(pieces),)),
        ],
        compiler_params=pltpu.CompilerParams(vmem_limit_bytes=40 << 20),
        name="attend",
    )(where, lengths, queries, *pieces)


def dot(a, b):
    return jnp.dot(a, b, preferred_element_type=jnp.float32)


def project(normed, parts):
    chunk, b1, f2, b2, f1 = parts
    width, half = chunk.shape[0], chunk.shape[0] // 2
    total = dot(normed[:, :width], chunk)
    total = total + dot(normed[:, width:2 * width], b1)
    total = total + dot(normed[:, 3 * width:], f1)
    total = total + dot(normed[:, 2 * width:2 * width + half], f2)
    total = total + dot(normed[:, 2 * width + half:3 * width], b2)
    return total.astype(jnp.bfloat16)


def shards(tokens, lengths, w_query, w_key, value_weight, w_out):
    ctx = lax.axis_index("ctx")
    y = lax.axis_index("dp")
    x = lax.axis_index("tp")
    z, core = ctx // 2, ctx % 2
    first = core == 0
    where = jnp.stack([y, z, core]).astype(jnp.int32)

    def pair_piece(a, b):
        mine, give = jnp.where(first, a, b), jnp.where(first, b, a)
        got = swap(give)
        return jnp.concatenate([jnp.where(first, mine, got), jnp.where(first, got, mine)], axis=0)

    kv_piece = pair_piece(w_key, value_weight)
    half = w_query.shape[1] // 2
    q_piece = pair_piece(w_query[:, :half], w_query[:, half:])
    normed = norm(tokens, where)
    kv_parts = ring4(z_gather(kv_piece), "dp")
    kv_other = tuple(swap(part) for part in kv_parts)
    q_parts = ring4(z_gather(q_piece), "dp")
    q_other = tuple(swap(part) for part in q_parts)
    kv_mine, kv_sib = project(normed, kv_parts), project(normed, kv_other)
    keys, values = jnp.where(first, kv_mine, kv_sib), jnp.where(first, kv_sib, kv_mine)

    pieces = []
    k, v = keys, values
    for dz in range(BACK + 1):
        if dz:
            k, v = z_shift(k, 1, False), z_shift(v, 1, False)
        pieces += [k, v, swap(k), swap(v)]

    q_mine, q_sib = project(normed, q_parts), project(normed, q_other)
    queries = jnp.concatenate([jnp.where(first, q_mine, q_sib), jnp.where(first, q_sib, q_mine)], axis=1)
    heads = attend(where, lengths, queries, pieces)

    own, b1, f2, b2, f1 = ring4(heads, "tp")
    width = heads.shape[1]

    def out_rows(dx):
        return lax.dynamic_slice_in_dim(w_out, lax.rem(x + dx, NX) * width, width, 0)

    total = dot(own, out_rows(0)) + dot(b1, out_rows(1)) + dot(f1, out_rows(3))
    total = total + dot(jnp.concatenate([f2, b2], axis=0), out_rows(2))
    return total.astype(jnp.bfloat16)


def solution(mesh):
    in_specs = (
        P(("dp", "ctx"), None),
        P("dp", None),
        P(("dp", "ctx"), "tp"),
        P(("dp", "ctx"), "tp"),
        P(("dp", "ctx"), "tp"),
        P(None, "tp"),
    )
    out_specs = P(("dp", "ctx"), "tp")
    return jax.shard_map(shards, mesh=mesh, in_specs=in_specs, out_specs=out_specs, check_vma=False)
```

```python
import functools

import jax
import jax.numpy as jnp
from jax import lax
from jax.experimental import pallas as pl
from jax.experimental.pallas import tpu as pltpu
from jax.sharding import PartitionSpec as P

HEAD = 128
GROUP = 4
EPSILON = 1e-05
MASKED = -1e30
LOG2E = 1.4426950408889634
NZ = 8
NY = 4
NX = 4
BACK = 4
ROWS = 512
CHIP = 2 * ROWS
BLOCK = 512
DOCS = 8


def z_shift(x, step):
    return lax.ppermute(x, "ctx", [(c, (c + 2 * step) % (2 * NZ)) for c in range(2 * NZ)])


def swap(x):
    return lax.ppermute(x, "ctx", [(c, c ^ 1) for c in range(2 * NZ)])


def shift(x, axis, step, n):
    return lax.ppermute(x, axis, [(i, (i + step) % n) for i in range(n)])


def everyone(x, axis, n, groups=None):
    spread = jnp.broadcast_to(x[None], (n,) + x.shape)
    got = lax.all_to_all(spread, axis, 0, 0, axis_index_groups=groups)
    return got.reshape((n * x.shape[0],) + x.shape[1:])


def ring4(chunk, axis):
    half = chunk.shape[0] // 2
    f1, b1 = shift(chunk, axis, 1, 4), shift(chunk, axis, -1, 4)
    f2, b2 = shift(f1[:half], axis, 1, 4), shift(b1[half:], axis, -1, 4)
    return chunk, b1, f2, b2, f1


def norm_kernel(x_ref, o_ref, p_ref):
    x = x_ref[...].astype(jnp.float32)
    scale = lax.rsqrt(jnp.mean(x * x, axis=1, keepdims=True) + EPSILON)
    normed = x * scale
    o_ref[...] = normed.astype(jnp.bfloat16)
    low = lax.broadcasted_iota(jnp.int32, (x.shape[0], 128), 1) < 64
    for ctx in range(2 * NZ):
        for pair in range(NY // 2):
            a, b = (
                normed[:, (dp * NZ + ctx // 2) * 128:(dp * NZ + ctx // 2 + 1) * 128]
                for dp in (2 * pair, 2 * pair + 1)
            )
            if ctx % 2:
                a = pltpu.roll(a, 64, 1)
            else:
                b = pltpu.roll(b, 64, 1)
            out = (ctx * 2 + pair) * 128
            p_ref[:, out:out + 128] = jnp.where(low, a, b).astype(jnp.bfloat16)


def norm(tokens):
    rows, width = tokens.shape
    tile = 64
    spec = pl.BlockSpec((tile, width), lambda i: (i, 0))
    return pl.pallas_call(
        norm_kernel,
        out_shape=[jax.ShapeDtypeStruct((rows, width), jnp.bfloat16)] * 2,
        grid=(rows // tile,),
        in_specs=[spec],
        out_specs=[spec, spec],
        compiler_params=pltpu.CompilerParams(vmem_limit_bytes=24 << 20),
        name="norm",
    )(tokens)


def attend_kernel(far, near, heads, begin, end, where_ref, lengths_ref, q_ref, *refs):
    chips = far - near + 1
    pieces, refs = refs[:2 * chips], refs[2 * chips:]
    if not begin:
        (ml_in, acc_in), refs = refs[:2], refs[2:]
    if end:
        (o_ref,), refs = refs[:1], refs[1:]
    pairs = (len(heads) + 1) // 2
    ml_refs, acc_refs, refs = refs[:pairs], refs[pairs:2 * pairs], refs[2 * pairs:]
    k_win, v_win, start_ref, sems = refs
    core, z = where_ref[1], where_ref[0]
    copies = []
    for i in range(chips):
        for which in range(2):
            side = core if which == 0 else 1 - core
            block = (chips - 1 - i) * 2 + side
            piece, sem = pieces[2 * i + which], (2 * i + which) * 5
            copies.append(pltpu.make_async_copy(piece.at[pl.ds(0, BLOCK), :], k_win.at[block], sems.at[sem]))
            for tile in range(BLOCK // HEAD):
                cols = pl.ds(tile * HEAD, HEAD)
                copies.append(
                    pltpu.make_async_copy(
                        piece.at[pl.ds(BLOCK + tile * HEAD, HEAD), :],
                        v_win.at[block, :, cols],
                        sems.at[sem + 1 + tile],
                    )
                )
    for copy in copies:
        copy.start()
    low, high = BACK - far, BACK - near + 1
    base = (z - BACK) * CHIP
    factor = HEAD ** (-0.5) * LOG2E
    first = BACK * CHIP + core * ROWS

    def start_of(pos, start):
        stop = jnp.int32(0)
        for d in range(DOCS):
            stop = stop + lengths_ref[0, d]
            start = jnp.where(stop <= pos, stop, start)
        return start - base

    pos = first + base + lax.broadcasted_iota(jnp.int32, start_ref.shape, 1)
    start_ref[...] = start_of(pos, jnp.zeros_like(pos))
    oldest = start_of(first + base, jnp.int32(0))
    newest = start_of(first + ROWS - 1 + base, jnp.int32(0))
    if begin:
        for ml_ref, acc_ref in zip(ml_refs, acc_refs):
            is_max = lax.broadcasted_iota(jnp.int32, ml_ref.shape, 0) < 2
            ml_ref[...] = jnp.where(is_max, MASKED, 0.0)
            acc_ref[...] = jnp.zeros_like(acc_ref)
    else:
        ml_refs[0][...] = ml_in[...]
        acc_refs[0][...] = acc_in[...]
    for copy in copies:
        copy.wait()

    def step(chip, masked):
        count, sides = range(len(heads)), range(2)
        scores = [
            [
                lax.dot_general(
                    k_win[2 * (chip - low) + side],
                    q_ref[:, h * HEAD:(h + 1) * HEAD],
                    (((1,), (1,)), ((), ())),
                    preferred_element_type=jnp.float32,
                )
                for side in sides
            ]
            for h in heads
        ]
        if masked:
            query = first + lax.broadcasted_iota(jnp.int32, (BLOCK, ROWS), 1)
            for side in sides:
                key = chip * CHIP + side * BLOCK + lax.broadcasted_iota(jnp.int32, (BLOCK, ROWS), 0)
                allowed = (key <= query) & (key >= start_ref[0:1, :])
                for i in count:
                    scores[i][side] = jnp.where(allowed, scores[i][side], MASKED)
        olds = [ml_refs[i // 2][i % 2:i % 2 + 1, :] for i in count]
        sums = [ml_refs[i // 2][2 + i % 2:3 + i % 2, :] for i in count]
        news, decays, blended = [], [], []
        for i in count:
            top = [jnp.max(s, axis=0, keepdims=True) for s in scores[i]]
            news.append(jnp.maximum(olds[i], jnp.maximum(top[0], top[1])))
            decays.append(jnp.exp2((olds[i] - news[i]) * factor))
        for i in count:
            ps = [jnp.exp2((s - news[i]) * factor) for s in scores[i]]
            sums[i] = sums[i] * decays[i] + sum(jnp.sum(p, axis=0, keepdims=True) for p in ps)
            parts = [
                jnp.dot(
                    v_win[2 * (chip - low) + side],
                    ps[side].astype(jnp.bfloat16),
                    preferred_element_type=jnp.float32,
                )
                for side in sides
            ]
            blended.append(parts[0] + parts[1])
        for i in count:
            ml_refs[i // 2][i % 2:i % 2 + 1, :] = news[i]
            ml_refs[i // 2][2 + i % 2:3 + i % 2, :] = sums[i]
            acc_refs[i // 2][i % 2] = acc_refs[i // 2][i % 2] * decays[i] + blended[i]

    def body(chip, carry):
        needs = (chip == BACK) | (chip * CHIP < newest)

        @pl.when(needs)
        def _():
            step(chip, True)

        @pl.when(jnp.logical_not(needs))
        def _():
            step(chip, False)

        return carry

    lax.fori_loop(jnp.maximum(oldest // CHIP, low), high, body, 0)
    if end:
        for i in range(2):
            out = acc_refs[0][i] / ml_refs[0][2 + i:3 + i, :]
            o_ref[:, i * HEAD:(i + 1) * HEAD] = out.T.astype(jnp.bfloat16)


def attend(where, lengths, queries, pieces, far, near, heads, state=None):
    begin, end = not state, far == BACK
    chips = far - near + 1
    vmem, smem = pl.BlockSpec(memory_space=pltpu.VMEM), pl.BlockSpec(memory_space=pltpu.SMEM)
    pairs = len(heads) // 2
    kept = [jax.ShapeDtypeStruct((8, ROWS), jnp.float32)] * pairs
    kept += [jax.ShapeDtypeStruct((2, HEAD, ROWS), jnp.float32)] * pairs
    scratch = [
        pltpu.VMEM((2 * chips, BLOCK, HEAD), jnp.bfloat16),
        pltpu.VMEM((2 * chips, HEAD, BLOCK), jnp.bfloat16),
        pltpu.VMEM((8, ROWS), jnp.int32),
        pltpu.SemaphoreType.DMA((10 * chips,)),
    ]
    if end:
        scratch = [pltpu.VMEM(s.shape, s.dtype) for s in kept] + scratch
    out = jax.ShapeDtypeStruct((ROWS, len(heads) * HEAD), jnp.bfloat16)
    return pl.pallas_call(
        functools.partial(attend_kernel, far, near, heads, begin, end),
        out_shape=out if end else kept,
        in_specs=[smem, smem, vmem]
        + [pl.BlockSpec(memory_space=pl.ANY)] * len(pieces)
        + [vmem] * len(state or ()),
        out_specs=vmem if end else [vmem] * len(kept),
        scratch_shapes=scratch,
        cost_estimate=pl.CostEstimate(
            flops=chips * 2 * ROWS * BLOCK * len(heads) * HEAD * 4,
            bytes_accessed=3 << 20,
            transcendentals=0,
        ),
        compiler_params=pltpu.CompilerParams(vmem_limit_bytes=40 << 20),
        name="attend%d" % far,
    )(where, lengths, queries, *pieces, *(state or ()))


def dot(a, b):
    return jnp.dot(a, b, preferred_element_type=jnp.float32)


def shards(tokens, lengths, w_query, w_key, value_weight, w_out):
    ctx = lax.axis_index("ctx")
    x = lax.axis_index("tp")
    z, core = ctx // 2, ctx % 2
    first = core == 0
    where = jnp.stack([z, core]).astype(jnp.int32)

    wq = everyone(w_query, "dp", NY)
    wq, w_key, value_weight = lax.optimization_barrier((wq, w_key, value_weight))
    wq = lax.all_gather(wq, "ctx", axis=0, tiled=True)
    got = swap(jnp.where(first, value_weight, w_key))
    piece = jnp.where(
        first,
        jnp.concatenate([w_key, got], axis=0),
        jnp.concatenate([got, value_weight], axis=0),
    )
    cores = [[2 * i + c for i in range(NZ)] for c in range(2)]
    kv = everyone(piece, "ctx", NZ, cores)
    normed, normed_moved = norm(tokens)
    kv, normed, normed_moved = lax.optimization_barrier((kv, normed, normed_moved))
    kv = everyone(kv, "dp", NY)
    kv_other = swap(kv)
    mine, other = dot(normed, kv).astype(jnp.bfloat16), dot(normed, kv_other).astype(jnp.bfloat16)
    keys, values = jnp.where(first, mine, other), jnp.where(first, other, mine)
    values = jnp.swapaxes(values.reshape(BLOCK // HEAD, HEAD, HEAD), 1, 2).reshape(BLOCK, HEAD)
    sent = jnp.concatenate([keys, values], axis=0)

    pieces = [sent, swap(sent)]
    sent = z_shift(sent, 1)
    queries = dot(normed_moved, wq).astype(jnp.bfloat16)
    sent, queries = lax.optimization_barrier((sent, queries))
    pieces += [sent, swap(sent)]
    states, later = [], []
    for i in range(2):
        sent = z_shift(sent, 1)
        state = attend(where, lengths, queries, pieces, 1, 0, range(2 * i, 2 * i + 2))
        sent, state = lax.optimization_barrier((sent, state))
        states.append(state)
        later += [sent, swap(sent)]
    sent = z_shift(sent, 1)
    later += [sent, swap(sent)]
    width, part = GROUP * HEAD, 2 * HEAD
    total = 0.0
    for i in range(2):
        mine = attend(where, lengths, queries, later, BACK, 2, range(2 * i, 2 * i + 2), states[i])
        own, b1, f2, b2, f1 = ring4(mine, "tp")
        around = (own, b1, jnp.concatenate([f2, b2], axis=0), f1)
        for dx in (0, 1, 3, 2):
            at = lax.rem(x + dx, NX) * width + i * part
            total = total + dot(around[dx], lax.dynamic_slice_in_dim(w_out, at, part, 0))
    return total.astype(jnp.bfloat16)


def solution(mesh):
    in_specs = (
        P(("dp", "ctx"), None),
        P("dp", None),
        P(("dp", "ctx"), "tp"),
        P(("dp", "ctx"), "tp"),
        P(("dp", "ctx"), "tp"),
        P(None, "tp"),
    )
    out_specs = P(("dp", "ctx"), "tp")
    return jax.shard_map(shards, mesh=mesh, in_specs=in_specs, out_specs=out_specs, check_vma=False)
```

```python
import functools

import jax
import jax.numpy as jnp
from jax import lax
from jax.experimental import pallas as pl
from jax.experimental.pallas import tpu as pltpu
from jax.sharding import PartitionSpec as P

HEAD = 128
GROUP = 4
EPSILON = 1e-05
MASKED = -1e30
LOG2E = 1.4426950408889634
NZ = 8
NY = 4
NX = 4
BACK = 4
ROWS = 512
CHIP = 2 * ROWS
BLOCK = 512
DOCS = 8


def z_shift(x, step):
    return lax.ppermute(x, "ctx", [(c, (c + 2 * step) % (2 * NZ)) for c in range(2 * NZ)])


def swap(x):
    return lax.ppermute(x, "ctx", [(c, c ^ 1) for c in range(2 * NZ)])


def shift(x, axis, step, n):
    return lax.ppermute(x, axis, [(i, (i + step) % n) for i in range(n)])


def everyone(x, axis, n, groups=None):
    spread = jnp.broadcast_to(x[None], (n,) + x.shape)
    got = lax.all_to_all(spread, axis, 0, 0, axis_index_groups=groups)
    return got.reshape((n * x.shape[0],) + x.shape[1:])


def norm_kernel(where_ref, x_ref, o_ref):
    x = x_ref[...].astype(jnp.float32)
    scale = lax.rsqrt(jnp.mean(x * x, axis=1, keepdims=True) + EPSILON)
    y, per = where_ref[2], NZ * 128
    for dy in range(NY):
        cols = pl.ds(pl.multiple_of(lax.rem(y + dy, NY) * per, per), per)
        moved = x_ref[:, cols].astype(jnp.float32) * scale
        o_ref[:, dy * per:(dy + 1) * per] = moved.astype(jnp.bfloat16)


def norm(tokens, where):
    rows, width = tokens.shape
    tile = 64
    spec = pl.BlockSpec((tile, width), lambda i: (i, 0))
    return pl.pallas_call(
        norm_kernel,
        out_shape=jax.ShapeDtypeStruct((rows, width), jnp.bfloat16),
        grid=(rows // tile,),
        in_specs=[pl.BlockSpec(memory_space=pltpu.SMEM), spec],
        out_specs=spec,
        compiler_params=pltpu.CompilerParams(vmem_limit_bytes=24 << 20),
        name="norm",
    )(where, tokens)


def attend_kernel(far, near, heads, begin, end, where_ref, lengths_ref, q_ref, *refs):
    chips = far - near + 1
    pieces, refs = refs[:2 * chips], refs[2 * chips:]
    if not begin:
        (ml_in, acc_in), refs = refs[:2], refs[2:]
    if end:
        (o_ref,), refs = refs[:1], refs[1:]
    pairs = (len(heads) + 1) // 2
    ml_refs, acc_refs, refs = refs[:pairs], refs[pairs:2 * pairs], refs[2 * pairs:]
    win, start_ref, sems = refs
    core, z = where_ref[1], where_ref[0]
    copies = []
    for i in range(chips):
        for which in range(2):
            side = core if which == 0 else 1 - core
            block = (chips - 1 - i) * 2 + side
            at = 2 * i + which
            copies.append(pltpu.make_async_copy(pieces[at], win.at[block], sems.at[at]))
    for copy in copies:
        copy.start()
    low, high = BACK - far, BACK - near + 1
    base = (z - BACK) * CHIP
    factor = HEAD ** (-0.5) * LOG2E
    first = BACK * CHIP + core * ROWS

    def start_of(pos, start):
        stop = jnp.int32(0)
        for d in range(DOCS):
            stop = stop + lengths_ref[0, d]
            start = jnp.where(stop <= pos, stop, start)
        return start - base

    pos = first + base + lax.broadcasted_iota(jnp.int32, start_ref.shape, 1)
    start_ref[...] = start_of(pos, jnp.zeros_like(pos))
    oldest = start_of(first + base, jnp.int32(0))
    newest = start_of(first + ROWS - 1 + base, jnp.int32(0))
    if begin:
        for ml_ref, acc_ref in zip(ml_refs, acc_refs):
            is_max = lax.broadcasted_iota(jnp.int32, ml_ref.shape, 0) < 2
            ml_ref[...] = jnp.where(is_max, MASKED, 0.0)
            acc_ref[...] = jnp.zeros_like(acc_ref)
    else:
        ml_refs[0][...] = ml_in[...]
        acc_refs[0][...] = acc_in[...]
    for copy in copies:
        copy.wait()

    def values_of(block):
        tiles = [win[block, BLOCK + i * HEAD:BLOCK + (i + 1) * HEAD, :] for i in range(BLOCK // HEAD)]
        return jnp.concatenate(tiles, axis=1)

    def step(chip, masked):
        count, sides = range(len(heads)), range(2)
        scores = [
            [
                lax.dot_general(
                    win[2 * (chip - low) + side, :BLOCK, :],
                    q_ref[:, h * HEAD:(h + 1) * HEAD],
                    (((1,), (1,)), ((), ())),
                    preferred_element_type=jnp.float32,
                )
                for side in sides
            ]
            for h in heads
        ]
        if masked:
            query = first + lax.broadcasted_iota(jnp.int32, (BLOCK, ROWS), 1)
            for side in sides:
                key = chip * CHIP + side * BLOCK + lax.broadcasted_iota(jnp.int32, (BLOCK, ROWS), 0)
                allowed = (key <= query) & (key >= start_ref[0:1, :])
                for i in count:
                    scores[i][side] = jnp.where(allowed, scores[i][side], MASKED)
        olds = [ml_refs[i // 2][i % 2:i % 2 + 1, :] for i in count]
        sums = [ml_refs[i // 2][2 + i % 2:3 + i % 2, :] for i in count]
        news, decays, blended = [], [], []
        for i in count:
            top = [jnp.max(s, axis=0, keepdims=True) for s in scores[i]]
            news.append(jnp.maximum(olds[i], jnp.maximum(top[0], top[1])))
            decays.append(jnp.exp2((olds[i] - news[i]) * factor))
        for i in count:
            ps = [jnp.exp2((s - news[i]) * factor) for s in scores[i]]
            sums[i] = sums[i] * decays[i] + sum(jnp.sum(p, axis=0, keepdims=True) for p in ps)
            parts = [
                jnp.dot(
                    values_of(2 * (chip - low) + side),
                    ps[side].astype(jnp.bfloat16),
                    preferred_element_type=jnp.float32,
                )
                for side in sides
            ]
            blended.append(parts[0] + parts[1])
        for i in count:
            ml_refs[i // 2][i % 2:i % 2 + 1, :] = news[i]
            ml_refs[i // 2][2 + i % 2:3 + i % 2, :] = sums[i]
            acc_refs[i // 2][i % 2] = acc_refs[i // 2][i % 2] * decays[i] + blended[i]

    def body(chip, carry):
        needs = (chip == BACK) | (chip * CHIP < newest)

        @pl.when(needs)
        def _():
            step(chip, True)

        @pl.when(jnp.logical_not(needs))
        def _():
            step(chip, False)

        return carry

    lax.fori_loop(jnp.maximum(oldest // CHIP, low), high, body, 0)
    if end:
        for i in range(2):
            out = acc_refs[0][i] / ml_refs[0][2 + i:3 + i, :]
            o_ref[:, i * HEAD:(i + 1) * HEAD] = out.T.astype(jnp.bfloat16)


def attend(where, lengths, queries, pieces, far, near, heads, state=None):
    begin, end = not state, far == BACK
    chips = far - near + 1
    vmem, smem = pl.BlockSpec(memory_space=pltpu.VMEM), pl.BlockSpec(memory_space=pltpu.SMEM)
    pairs = len(heads) // 2
    kept = [jax.ShapeDtypeStruct((8, ROWS), jnp.float32)] * pairs
    kept += [jax.ShapeDtypeStruct((2, HEAD, ROWS), jnp.float32)] * pairs
    scratch = [
        pltpu.VMEM((2 * chips, 2 * BLOCK, HEAD), jnp.bfloat16),
        pltpu.VMEM((8, ROWS), jnp.int32),
        pltpu.SemaphoreType.DMA((2 * chips,)),
    ]
    if end:
        scratch = [pltpu.VMEM(s.shape, s.dtype) for s in kept] + scratch
    out = jax.ShapeDtypeStruct((ROWS, len(heads) * HEAD), jnp.bfloat16)
    return pl.pallas_call(
        functools.partial(attend_kernel, far, near, heads, begin, end),
        out_shape=out if end else kept,
        in_specs=[smem, smem, vmem]
        + [pl.BlockSpec(memory_space=pl.ANY)] * len(pieces)
        + [vmem] * len(state or ()),
        out_specs=vmem if end else [vmem] * len(kept),
        scratch_shapes=scratch,
        cost_estimate=pl.CostEstimate(
            flops=chips * 2 * ROWS * BLOCK * len(heads) * HEAD * 4,
            bytes_accessed=3 << 20,
            transcendentals=0,
        ),
        compiler_params=pltpu.CompilerParams(vmem_limit_bytes=40 << 20),
        name="attend%d" % far,
    )(where, lengths, queries, *pieces, *(state or ()))


def dot(a, b):
    return jnp.dot(a, b, preferred_element_type=jnp.float32)


def shards(tokens, lengths, w_query, w_key, value_weight, w_out):
    ctx = lax.axis_index("ctx")
    x = lax.axis_index("tp")
    z, core = ctx // 2, ctx % 2
    first = core == 0
    where = jnp.stack([z, core, lax.axis_index("dp")]).astype(jnp.int32)

    def halves(a, b):
        got = swap(jnp.where(first, b, a))
        return jnp.where(
            first, jnp.concatenate([a, got], axis=0), jnp.concatenate([got, b], axis=0)
        )

    cores = [[2 * i + c for i in range(NZ)] for c in range(2)]
    half = w_query.shape[1] // 2
    piece = halves(
        jnp.concatenate([w_key, w_query[:, :half]], axis=1),
        jnp.concatenate([value_weight, w_query[:, half:]], axis=1),
    )
    gathered = everyone(piece, "ctx", NZ, cores)
    normed = norm(tokens, where)

    def from_y(weights):
        return [weights] + [shift(weights, "dp", -dy, NY) for dy in range(1, NY)]

    def project(parts):
        width = parts[0].shape[0]
        mine = other = 0.0
        for dy in (0, 1, 3, 2):
            cols = normed[:, dy * width:(dy + 1) * width]
            mine, other = mine + dot(cols, parts[dy]), other + dot(cols, swap(parts[dy]))
        mine, other = mine.astype(jnp.bfloat16), other.astype(jnp.bfloat16)
        return jnp.where(first, mine, other), jnp.where(first, other, mine)

    kv, wq = gathered[:, :HEAD], gathered[:, HEAD:]
    kv, wq = lax.optimization_barrier((from_y(kv), wq))
    keys, values = project(kv)
    near = [shift(wq, "dp", -1, NY), shift(wq, "dp", 1, NY)]
    middle = wq.shape[0] // 2
    opposite = [shift(near[0][:middle], "dp", -1, NY), shift(near[1][middle:], "dp", 1, NY)]
    wq = [wq, near[0], jnp.concatenate(opposite, axis=0), near[1]]
    values = jnp.swapaxes(values.reshape(BLOCK // HEAD, HEAD, HEAD), 1, 2).reshape(BLOCK, HEAD)
    sent = jnp.concatenate([keys, values], axis=0)

    pieces = [sent, swap(sent)]
    sent = z_shift(sent, 1)
    pieces += [sent, swap(sent)]
    sent = z_shift(sent, 1)
    queries = jnp.concatenate(project(wq), axis=1)
    states, later = [], [sent, swap(sent)]
    for i in range(2):
        sent = z_shift(sent, 1)
        state = attend(where, lengths, queries, pieces, 1, 0, range(2 * i, 2 * i + 2))
        sent, state = lax.optimization_barrier((sent, state))
        states.append(state)
        later += [sent, swap(sent)]
    width, part = GROUP * HEAD, 2 * HEAD
    total = 0.0
    for i in range(2):
        mine = attend(where, lengths, queries, later, BACK, 2, range(2 * i, 2 * i + 2), states[i])
        near = [shift(mine, "tp", -1, NX), shift(mine, "tp", 1, NX)]
        if i == 0:
            opposite = shift(mine, "tp", 2, NX)
        else:
            half = ROWS // 2
            opposite = jnp.concatenate(
                [shift(near[0][:half], "tp", -1, NX), shift(near[1][half:], "tp", 1, NX)], axis=0
            )
        around = [mine, near[0], opposite, near[1]]
        for dx in (0, 1, 3, 2):
            at = lax.rem(x + dx, NX) * width + i * part
            total = total + dot(around[dx], lax.dynamic_slice_in_dim(w_out, at, part, 0))
    return total.astype(jnp.bfloat16)


def solution(mesh):
    in_specs = (
        P(("dp", "ctx"), None),
        P("dp", None),
        P(("dp", "ctx"), "tp"),
        P(("dp", "ctx"), "tp"),
        P(("dp", "ctx"), "tp"),
        P(None, "tp"),
    )
    out_specs = P(("dp", "ctx"), "tp")
    return jax.shard_map(shards, mesh=mesh, in_specs=in_specs, out_specs=out_specs, check_vma=False)
```

```python
import functools

import jax
import jax.numpy as jnp
from jax import lax
from jax.experimental import pallas as pl
from jax.experimental.pallas import tpu as pltpu
from jax.sharding import PartitionSpec as P

HEAD = 128
GROUP = 4
EPSILON = 1e-05
MASKED = -1e30
LOG2E = 1.4426950408889634
NZ = 8
NY = 4
NX = 4
BACK = 4
ROWS = 512
CHIP = 2 * ROWS
BLOCK = 512
DOCS = 8


def z_shift(x, step):
    return lax.ppermute(x, "ctx", [(c, (c + 2 * step) % (2 * NZ)) for c in range(2 * NZ)])


def swap(x):
    return lax.ppermute(x, "ctx", [(c, c ^ 1) for c in range(2 * NZ)])


def shift(x, axis, step, n):
    return lax.ppermute(x, axis, [(i, (i + step) % n) for i in range(n)])


def everyone(x, axis, n, groups=None):
    spread = jnp.broadcast_to(x[None], (n,) + x.shape)
    got = lax.all_to_all(spread, axis, 0, 0, axis_index_groups=groups)
    return got.reshape((n * x.shape[0],) + x.shape[1:])


def norm_kernel(where_ref, x_ref, o_ref):
    x = x_ref[...].astype(jnp.float32)
    scale = lax.rsqrt(jnp.mean(x * x, axis=1, keepdims=True) + EPSILON)
    y, per = where_ref[2], NZ * 128
    for dy in range(NY):
        cols = pl.ds(pl.multiple_of(lax.rem(y + dy, NY) * per, per), per)
        moved = x_ref[:, cols].astype(jnp.float32) * scale
        o_ref[:, dy * per:(dy + 1) * per] = moved.astype(jnp.bfloat16)


def norm(tokens, where):
    rows, width = tokens.shape
    tile = 64
    spec = pl.BlockSpec((tile, width), lambda i: (i, 0))
    return pl.pallas_call(
        norm_kernel,
        out_shape=jax.ShapeDtypeStruct((rows, width), jnp.bfloat16),
        grid=(rows // tile,),
        in_specs=[pl.BlockSpec(memory_space=pltpu.SMEM), spec],
        out_specs=spec,
        compiler_params=pltpu.CompilerParams(vmem_limit_bytes=24 << 20),
        name="norm",
    )(where, tokens)


def attend_kernel(far, near, heads, begin, end, where_ref, lengths_ref, q_ref, *refs):
    chips = far - near + 1
    pieces, refs = refs[:2 * chips], refs[2 * chips:]
    if not begin:
        (ml_in, acc_in), refs = refs[:2], refs[2:]
    if end:
        (o_ref,), refs = refs[:1], refs[1:]
    pairs = (len(heads) + 1) // 2
    ml_refs, acc_refs, refs = refs[:pairs], refs[pairs:2 * pairs], refs[2 * pairs:]
    win, start_ref, sems = refs
    core, z = where_ref[1], where_ref[0]
    copies = []
    for i in range(chips):
        for which in range(2):
            side = core if which == 0 else 1 - core
            block = (chips - 1 - i) * 2 + side
            at = 2 * i + which
            copies.append(pltpu.make_async_copy(pieces[at], win.at[block], sems.at[at]))
    for copy in copies:
        copy.start()
    low, high = BACK - far, BACK - near + 1
    base = (z - BACK) * CHIP
    factor = HEAD ** (-0.5) * LOG2E
    first = BACK * CHIP + core * ROWS

    def start_of(pos, start):
        stop = jnp.int32(0)
        for d in range(DOCS):
            stop = stop + lengths_ref[0, d]
            start = jnp.where(stop <= pos, stop, start)
        return start - base

    pos = first + base + lax.broadcasted_iota(jnp.int32, start_ref.shape, 1)
    start_ref[...] = start_of(pos, jnp.zeros_like(pos))
    oldest = start_of(first + base, jnp.int32(0))
    newest = start_of(first + ROWS - 1 + base, jnp.int32(0))
    if begin:
        for ml_ref, acc_ref in zip(ml_refs, acc_refs):
            is_max = lax.broadcasted_iota(jnp.int32, ml_ref.shape, 0) < 2
            ml_ref[...] = jnp.where(is_max, MASKED, 0.0)
            acc_ref[...] = jnp.zeros_like(acc_ref)
    else:
        ml_refs[0][...] = ml_in[...]
        acc_refs[0][...] = acc_in[...]
    for copy in copies:
        copy.wait()

    def values_of(block):
        tiles = [win[block, BLOCK + i * HEAD:BLOCK + (i + 1) * HEAD, :] for i in range(BLOCK // HEAD)]
        return jnp.concatenate(tiles, axis=1)

    def step(chip, masked):
        count, sides = range(len(heads)), range(2)
        scores = [
            [
                lax.dot_general(
                    win[2 * (chip - low) + side, :BLOCK, :],
                    q_ref[:, h * HEAD:(h + 1) * HEAD],
                    (((1,), (1,)), ((), ())),
                    preferred_element_type=jnp.float32,
                )
                for side in sides
            ]
            for h in heads
        ]
        if masked:
            query = first + lax.broadcasted_iota(jnp.int32, (BLOCK, ROWS), 1)
            for side in sides:
                key = chip * CHIP + side * BLOCK + lax.broadcasted_iota(jnp.int32, (BLOCK, ROWS), 0)
                allowed = (key <= query) & (key >= start_ref[0:1, :])
                for i in count:
                    scores[i][side] = jnp.where(allowed, scores[i][side], MASKED)
        olds = [ml_refs[i // 2][i % 2:i % 2 + 1, :] for i in count]
        sums = [ml_refs[i // 2][2 + i % 2:3 + i % 2, :] for i in count]
        news, decays, blended = [], [], []
        for i in count:
            top = [jnp.max(s, axis=0, keepdims=True) for s in scores[i]]
            news.append(jnp.maximum(olds[i], jnp.maximum(top[0], top[1])))
            decays.append(jnp.exp2((olds[i] - news[i]) * factor))
        for i in count:
            ps = [jnp.exp2((s - news[i]) * factor) for s in scores[i]]
            sums[i] = sums[i] * decays[i] + sum(jnp.sum(p, axis=0, keepdims=True) for p in ps)
            parts = [
                jnp.dot(
                    values_of(2 * (chip - low) + side),
                    ps[side].astype(jnp.bfloat16),
                    preferred_element_type=jnp.float32,
                )
                for side in sides
            ]
            blended.append(parts[0] + parts[1])
        for i in count:
            ml_refs[i // 2][i % 2:i % 2 + 1, :] = news[i]
            ml_refs[i // 2][2 + i % 2:3 + i % 2, :] = sums[i]
            acc_refs[i // 2][i % 2] = acc_refs[i // 2][i % 2] * decays[i] + blended[i]

    def body(chip, carry):
        needs = (chip == BACK) | (chip * CHIP < newest)

        @pl.when(needs)
        def _():
            step(chip, True)

        @pl.when(jnp.logical_not(needs))
        def _():
            step(chip, False)

        return carry

    lax.fori_loop(jnp.maximum(oldest // CHIP, low), high, body, 0)
    if end:
        for i in range(2):
            out = acc_refs[0][i] / ml_refs[0][2 + i:3 + i, :]
            o_ref[:, i * HEAD:(i + 1) * HEAD] = out.T.astype(jnp.bfloat16)


def attend(where, lengths, queries, pieces, far, near, heads, state=None):
    begin, end = not state, far == BACK
    chips = far - near + 1
    vmem, smem = pl.BlockSpec(memory_space=pltpu.VMEM), pl.BlockSpec(memory_space=pltpu.SMEM)
    pairs = len(heads) // 2
    kept = [jax.ShapeDtypeStruct((8, ROWS), jnp.float32)] * pairs
    kept += [jax.ShapeDtypeStruct((2, HEAD, ROWS), jnp.float32)] * pairs
    scratch = [
        pltpu.VMEM((2 * chips, 2 * BLOCK, HEAD), jnp.bfloat16),
        pltpu.VMEM((8, ROWS), jnp.int32),
        pltpu.SemaphoreType.DMA((2 * chips,)),
    ]
    if end:
        scratch = [pltpu.VMEM(s.shape, s.dtype) for s in kept] + scratch
    out = jax.ShapeDtypeStruct((ROWS, len(heads) * HEAD), jnp.bfloat16)
    return pl.pallas_call(
        functools.partial(attend_kernel, far, near, heads, begin, end),
        out_shape=out if end else kept,
        in_specs=[smem, smem, vmem]
        + [pl.BlockSpec(memory_space=pl.ANY)] * len(pieces)
        + [vmem] * len(state or ()),
        out_specs=vmem if end else [vmem] * len(kept),
        scratch_shapes=scratch,
        cost_estimate=pl.CostEstimate(
            flops=chips * 2 * ROWS * BLOCK * len(heads) * HEAD * 4,
            bytes_accessed=3 << 20,
            transcendentals=0,
        ),
        compiler_params=pltpu.CompilerParams(vmem_limit_bytes=40 << 20),
        name="attend%d" % far,
    )(where, lengths, queries, *pieces, *(state or ()))


def dot(a, b):
    return jnp.dot(a, b, preferred_element_type=jnp.float32)


def shards(tokens, lengths, w_query, w_key, value_weight, w_out):
    ctx = lax.axis_index("ctx")
    x = lax.axis_index("tp")
    z, core = ctx // 2, ctx % 2
    first = core == 0
    where = jnp.stack([z, core, lax.axis_index("dp")]).astype(jnp.int32)

    def halves(a, b):
        got = swap(jnp.where(first, b, a))
        return jnp.where(
            first, jnp.concatenate([a, got], axis=0), jnp.concatenate([got, b], axis=0)
        )

    cores = [[2 * i + c for i in range(NZ)] for c in range(2)]
    half = w_query.shape[1] // 2
    piece = halves(
        jnp.concatenate([w_key, w_query[:, :half]], axis=1),
        jnp.concatenate([value_weight, w_query[:, half:]], axis=1),
    )
    gathered = everyone(piece, "ctx", NZ, cores)
    normed = norm(tokens, where)

    def from_y(weights):
        return [weights] + [shift(weights, "dp", -dy, NY) for dy in range(1, NY)]

    def project(parts):
        width = parts[0].shape[0]
        mine = other = 0.0
        for dy in (0, 1, 3, 2):
            cols = normed[:, dy * width:(dy + 1) * width]
            mine, other = mine + dot(cols, parts[dy]), other + dot(cols, swap(parts[dy]))
        mine, other = mine.astype(jnp.bfloat16), other.astype(jnp.bfloat16)
        return jnp.where(first, mine, other), jnp.where(first, other, mine)

    kv, wq = gathered[:, :HEAD], gathered[:, HEAD:]
    keys, values = project(from_y(kv))
    values = jnp.swapaxes(values.reshape(BLOCK // HEAD, HEAD, HEAD), 1, 2).reshape(BLOCK, HEAD)
    sent = jnp.concatenate([keys, values], axis=0)

    sent, wq = lax.optimization_barrier((sent, wq))
    near = [shift(wq, "dp", -1, NY), shift(wq, "dp", 1, NY)]
    middle = wq.shape[0] // 2
    opposite = [shift(near[0][:middle], "dp", -1, NY), shift(near[1][middle:], "dp", 1, NY)]
    wq = [wq, near[0], jnp.concatenate(opposite, axis=0), near[1]]
    pieces = []
    for dz in range(BACK):
        if dz:
            sent = z_shift(sent, 1)
        pieces += [sent, swap(sent)]
    sent = z_shift(sent, 1)
    queries = jnp.concatenate(project(wq), axis=1)
    state = attend(where, lengths, queries, pieces[:4], 1, 0, range(GROUP))
    sent, state = lax.optimization_barrier((sent, state))
    later = pieces[4:] + [sent, swap(sent)]
    states = [(state[i], state[2 + i]) for i in range(2)]
    width, part = GROUP * HEAD, 2 * HEAD
    total = 0.0
    for i in range(2):
        mine = attend(where, lengths, queries, later, BACK, 2, range(2 * i, 2 * i + 2), states[i])
        near = [shift(mine, "tp", -1, NX), shift(mine, "tp", 1, NX)]
        if i == 0:
            opposite = shift(mine, "tp", 2, NX)
        else:
            half = ROWS // 2
            opposite = jnp.concatenate(
                [shift(near[0][:half], "tp", -1, NX), shift(near[1][half:], "tp", 1, NX)], axis=0
            )
        around = [mine, near[0], opposite, near[1]]
        for dx in (0, 1, 3, 2):
            at = lax.rem(x + dx, NX) * width + i * part
            total = total + dot(around[dx], lax.dynamic_slice_in_dim(w_out, at, part, 0))
    return total.astype(jnp.bfloat16)


def solution(mesh):
    in_specs = (
        P(("dp", "ctx"), None),
        P("dp", None),
        P(("dp", "ctx"), "tp"),
        P(("dp", "ctx"), "tp"),
        P(("dp", "ctx"), "tp"),
        P(None, "tp"),
    )
    out_specs = P(("dp", "ctx"), "tp")
    return jax.shard_map(shards, mesh=mesh, in_specs=in_specs, out_specs=out_specs, check_vma=False)
```
